32 devices in a mesh: rows: 8 (over z, y), rep: 4 (over x, core).
Axes of the slice: x: 2, y: 2, z: 4, core: 2. Of those that a mesh axis runs over, the one named last changes fastest.
Arguments:
- features: bfloat16 [32768, 128], P('rows'), may hold values from -6 to 6
- tile_values: bfloat16 [8, 4, 512, 128, 128], P('rows', 'rep'), may hold values from -0.25 to 0.25
- tile_rows: int32 [8, 4, 512], P('rows', 'rep'), may hold values from 0 to 31
- tile_slots: int32 [8, 4, 512], P('rows', 'rep'), may hold values from 0 to 63
- tile_counts: int32 [8, 4], P('rows', 'rep'), may hold values from 64 to 512, as said below
- fetch_lists: int32 [8, 8, 8], P('rows'), may hold values from 0 to 31, as said below
- filter_weights: bfloat16 [4, 128, 256], replicated, may hold values from -0.5 to 0.5
Outputs:
- convolved: bfloat16 [32768, 256], P(('rows', 'rep'))
The draws below stay inside these ranges and needn't reach their ends.
Inputs may be any that keep to these rules, and one draw needn't show every extreme that they name: Tile slots from tile_counts[r, j] on carry no part of the operator; one device has all 512 slots live. `fetch_lists`: the 8 entries of one reader and one owner are distinct.
All inputs are finite; a program needn't handle non-finite values.
Results may differ from the reference program's by a relative error of at most 0.0065.
Values may be sent and summed in bfloat16 or wider, within the bound.
A program may use at most 128 MiB of HBM per device.

```python
import jax
import jax.numpy as jnp
from jax import lax

F_IN = 128
F_OUT = 256
TILE = 128
DEGREE = 3
RB = 32
PER_PEER = 8
TMAX = 512
SLOTS = 64
NODES = 32768
N_ROWS = 8
N_REP = 4


def draw_tile_counts(key, part):
    base = jax.random.randint(key, (N_ROWS * N_REP,), TMAX // 8, TMAX // 2, dtype=jnp.int32)
    chosen = jax.random.randint(jax.random.fold_in(key, 1), (), 0, N_ROWS * N_REP, dtype=jnp.int32)
    filled = jnp.where(jnp.arange(N_ROWS * N_REP, dtype=jnp.int32) == chosen, TMAX, base)
    return filled.reshape(N_ROWS, N_REP).astype(jnp.int32)


def draw_fetch_lists(key, part):
    scores = jax.random.randint(key, (N_ROWS, N_ROWS, RB), 0, 1 << 20, dtype=jnp.int32)
    scores = scores * RB + jnp.arange(RB, dtype=jnp.int32)
    scores = scores.at[0, 0, 0].set(-2)
    scores = scores.at[0, 0, RB - 1].set(-1)
    order = jnp.argsort(scores, axis=-1, stable=True).astype(jnp.int32)
    return order[:, :, :PER_PEER]


def plant(drawn, stream_key, low, top_value):
    shape = drawn.shape
    spot = [jax.random.randint(jax.random.fold_in(stream_key, axis), (), 0, shape[axis]) for axis in range(len(shape))]
    drawn = drawn.at[tuple(spot)].set(low)
    longest = shape.index(max(shape))
    spot[longest] = (spot[longest] + 1) % shape[longest]
    return drawn.at[tuple(spot)].set(top_value)


def steps_of(stream_key, dims, shards, smallest, top_value):
    loudness = 1.0
    for position, shards_of in shards:
        draws = jax.random.uniform(jax.random.fold_in(jax.random.fold_in(stream_key, 6), position), (shards_of,), jnp.float32, smallest / len(shards), top_value / len(shards))
        loudness = loudness * jnp.repeat(jnp.exp(draws), dims[position] // shards_of).reshape((-1,) + (1,) * (len(dims) - 1 - position))
    return loudness


def normal_values(rng, dims, spread, most, cuts=(), held_as=jnp.bfloat16):
    array = spread * jax.random.normal(rng, dims, jnp.float32)
    if cuts:
        array = array * steps_of(rng, dims, cuts, -0.22, 0.18)
    return jnp.clip(array, -most, most).astype(held_as)


def setup_inputs(seed: int = 0) -> dict:
    seeds = jax.random.split(jax.random.key(seed), 8)
    return {
        "features": normal_values(seeds[0], (NODES, F_IN), 1.0, 6.0, ((0, 8),)),
        "tile_values": normal_values(seeds[1], (N_ROWS, N_REP, TMAX, TILE, TILE), ((TILE * N_REP * TMAX // RB // 3) ** -0.5), 0.25, ((0, 8), (1, 4))),
        "tile_rows": plant(jax.random.randint(seeds[2], (N_ROWS, N_REP, TMAX), 0, RB), jax.random.fold_in(seeds[2], 1), 0, RB - 1).astype(jnp.int32),
        "tile_slots": plant(jax.random.randint(seeds[3], (N_ROWS, N_REP, TMAX), 0, SLOTS), jax.random.fold_in(seeds[3], 1), 0, SLOTS - 1).astype(jnp.int32),
        "tile_counts": draw_tile_counts(jax.random.fold_in(seeds[7], 71), 0),
        "fetch_lists": draw_fetch_lists(jax.random.fold_in(seeds[7], 71), 0),
        "filter_weights": normal_values(seeds[6], (DEGREE + 1, F_IN, F_OUT), F_IN ** -0.5, 0.5),
    }


def gather_blocks(previous, wanted):
    blocks = previous.reshape(N_ROWS, RB, TILE, F_IN)
    owners = jnp.arange(N_ROWS, dtype=jnp.int32)[:, None]
    return blocks[owners, wanted].reshape(N_ROWS * PER_PEER, TILE, F_IN)


def replica_term(total, fetched, values, rows_of, slots_of, count):
    def one_block(number, running):
        start = number * 64
        part = lax.dynamic_slice_in_dim(values, start, 64, 0).astype(jnp.float32)
        rows_part = lax.dynamic_slice_in_dim(rows_of, start, 64, 0)
        slots_part = lax.dynamic_slice_in_dim(slots_of, start, 64, 0)
        picked = fetched[slots_part].astype(jnp.float32)
        product = jnp.einsum("tij,tjf->tif", part, picked)
        live = (start + jnp.arange(64, dtype=jnp.int32)) < count
        product = jnp.where(live[:, None, None], product, jnp.zeros_like(product))
        return running.at[rows_part].add(product)

    return lax.fori_loop(0, (count + 63) // 64, one_block, total)


def apply_operator(previous, tile_values, tile_rows, tile_slots, tile_counts, fetch_lists):
    def one_owner(inputs):
        values, rows_of, slots_of, counts, wanted = inputs
        fetched = gather_blocks(previous, wanted)
        total = jnp.zeros((RB, TILE, F_IN), jnp.float32)
        for replica in range(N_REP):
            total = replica_term(total, fetched, values[replica], rows_of[replica], slots_of[replica], counts[replica])
        return total

    result = lax.map(one_owner, (tile_values, tile_rows, tile_slots, tile_counts, fetch_lists))
    return result.reshape(NODES, F_IN)


def reference(features, tile_values, tile_rows, tile_slots, tile_counts, fetch_lists, filter_weights):
    terms = [features]
    for degree in range(1, DEGREE + 1):
        total = apply_operator(terms[-1], tile_values, tile_rows, tile_slots, tile_counts, fetch_lists)
        if degree == 1:
            following = total
        else:
            following = 2.0 * total - terms[-2].astype(jnp.float32)
        terms.append(following.astype(jnp.bfloat16))
    output = jnp.zeros((NODES, F_OUT), jnp.float32)
    for degree in range(DEGREE + 1):
        output = output + jnp.dot(terms[degree], filter_weights[degree], preferred_element_type=jnp.float32)
    return output.astype(jnp.bfloat16)
```

```python
import functools

import jax
import jax.numpy as jnp
from jax import lax
from jax.experimental import pallas as pl
from jax.experimental.pallas import tpu as pltpu
from jax.sharding import PartitionSpec as P

BATCH = 16
MESH = pl.DeviceIdType.MESH
F32, BF16 = jnp.float32, jnp.bfloat16


class Plan:
    def __init__(self, n_rows, n_rep, row_blocks, per_peer):
        self.n, self.reps, self.chips = n_rows, n_rep, n_rep // 2
        self.blocks, self.peer = row_blocks, per_peer
        self.share, self.portion = row_blocks // n_rep, per_peer // n_rep

    def place(self):
        self.r, self.j = lax.axis_index("rows"), lax.axis_index("rep")
        self.c, self.x = lax.rem(self.j, 2), lax.div(self.j, 2)
        self.sib = self.j + 1 - 2 * self.c

    def chip(self, e):
        return lax.rem(self.x + e + self.chips, self.chips)

    def rank(self, e):
        return self.chip(e) * 2 + self.c

    def row(self, d):
        return lax.rem(self.r + d + self.n, self.n)


def remote(src, dst, send, recv, target):
    copy = pltpu.make_async_remote_copy(
        src_ref=src, dst_ref=dst, send_sem=send, recv_sem=recv, device_id=target, device_id_type=MESH
    )
    copy.start()
    return copy


def greet(plan, with_rows):
    barrier = pltpu.get_barrier_semaphore()
    targets = [(plan.r, plan.sib)] + [(plan.r, plan.rank(e)) for e in range(1, plan.chips)]
    if with_rows:
        targets += [(plan.row(d), plan.j) for d in range(1, plan.n)]
    for target in targets:
        pl.semaphore_signal(barrier, inc=1, device_id=target, device_id_type=MESH)
    pl.semaphore_wait(barrier, len(targets))


def exchange(plan, full, served, fetched, stage, sems):
    ex, fx, fc = sems
    n, chips, portion, peer = plan.n, plan.chips, plan.portion, plan.peer
    sent, across, beside = {}, {}, {}
    for d in range(1, n):
        to = plan.row(d)
        for i in range(portion):
            stage[d - 1, i] = full[served[to, 0, plan.j * portion + i]]
        sent[d] = remote(
            stage.at[d - 1],
            fetched.at[pl.ds(plan.r * peer + plan.j * portion, portion)],
            ex.at[0, d],
            ex.at[1, d],
            (to, plan.j),
        )
    for s in range(peer):
        fetched[plan.r * peer + s] = full[served[plan.r, 0, s]]

    def segment(d, rank):
        return fetched.at[pl.ds(plan.row(-d) * peer + rank * portion, portion)]

    for d in range(1, n):
        sent[d].wait_recv()
        seg = segment(d, plan.j)
        for e in range(1, chips):
            across[d, e] = remote(seg, seg, fx.at[0, d, e], fx.at[1, d, e], (plan.r, plan.rank(e)))
        beside[d, 0] = remote(seg, seg, fc.at[0, d, 0], fc.at[1, d, 0], (plan.r, plan.sib))
    for d in range(1, n):
        for e in range(1, chips):
            across[d, e].wait_recv()
            seg = segment(d, plan.rank(-e))
            beside[d, e] = remote(seg, seg, fc.at[0, d, e], fc.at[1, d, e], (plan.r, plan.sib))
    for copy in beside.values():
        copy.wait_recv()
    for copies in (sent, across, beside):
        for copy in copies.values():
            copy.wait_send()


def first_kernel(plan, wanted, full, fetched, served, lists, stage, ls, ex, fx, fc, local):
    plan.place()
    greet(plan, True)
    copies = [
        remote(wanted.at[plan.row(d)], lists.at[plan.r], ls.at[0, d], ls.at[1, d], (plan.row(d), plan.j))
        for d in range(1, plan.n)
    ]
    lists[plan.r] = wanted[plan.r]
    for copy in copies:
        copy.wait_recv()
    inner = pltpu.make_async_copy(lists, served, local)
    inner.start()
    inner.wait()
    exchange(plan, full, served, fetched, stage, (ex, fx, fc))
    for copy in copies:
        copy.wait_send()


def reduce_share(plan, degree, partial, previous, core_in, chip_out, x_in, cs, xs, write):
    share, chips = plan.share, plan.chips
    core, cross = {}, {}
    for e in [*range(1, chips), 0]:
        core[e] = remote(
            partial.at[pl.ds((plan.chip(e) * 2 + 1 - plan.c) * share, share)],
            core_in.at[e],
            cs.at[0, e],
            cs.at[1, e],
            (plan.r, plan.sib),
        )
    for e in range(1, chips):
        core[e].wait_recv()

        @pl.loop(0, share)
        def _(b):
            chip_out[e - 1, b] = (partial[plan.rank(e) * share + b] + core_in[e, b]).astype(BF16)

        cross[e] = remote(
            chip_out.at[e - 1], x_in.at[e - 1], xs.at[0, e], xs.at[1, e], (plan.r, plan.rank(e))
        )
    core[0].wait_recv()
    for e in range(1, chips):
        cross[e].wait_recv()

    @pl.loop(0, share)
    def _(b):
        total = partial[plan.j * share + b] + core_in[0, b]
        for e in range(1, chips):
            total = total + x_in[e - 1, b].astype(F32)
        if degree > 1:
            total = 2.0 * total - previous[b].astype(F32)
        write(b, total.astype(BF16))

    return [*core.values(), *cross.values()]


def middle_kernel(
    plan, degree, partial, previous, served, fetched, own, core_in, chip_out, x_in, full, stage, cs, xs, ax, ac, ex, fx, fc
):
    plan.place()
    greet(plan, True)
    share, chips = plan.share, plan.chips

    def write(b, block):
        own[b] = block
        full[plan.j * share + b] = block

    pending = reduce_share(plan, degree, partial, previous, core_in, chip_out, x_in, cs, xs, write)
    part = full.at[pl.ds(plan.j * share, share)]
    across = {
        e: remote(part, part, ax.at[0, e], ax.at[1, e], (plan.r, plan.rank(e))) for e in range(1, chips)
    }
    beside = [remote(part, part, ac.at[0, 0], ac.at[1, 0], (plan.r, plan.sib))]
    for e in range(1, chips):
        across[e].wait_recv()
        part = full.at[pl.ds(plan.rank(-e) * share, share)]
        beside.append(remote(part, part, ac.at[0, e], ac.at[1, e], (plan.r, plan.sib)))
    for copy in beside:
        copy.wait_recv()
    exchange(plan, full, served, fetched, stage, (ex, fx, fc))
    for copy in [*pending, *across.values(), *beside]:
        copy.wait_send()


def last_kernel(plan, degree, partial, previous, own, core_in, chip_out, x_in, cs, xs):
    plan.place()
    greet(plan, False)

    def write(b, block):
        own[b] = block

    for copy in reduce_share(plan, degree, partial, previous, core_in, chip_out, x_in, cs, xs, write):
        copy.wait_send()


def tile_kernel(row_blocks, count, rows_of, slots_of, values, fetched, total):
    step = pl.program_id(0)
    start = step * BATCH

    @pl.when(step == 0)
    def _():
        @pl.loop(0, row_blocks + 1)
        def _(b):
            total[b] = jnp.zeros(total.shape[1:], F32)

    @pl.when(start < count[0])
    def _():
        for i in range(BATCH):
            product = jnp.dot(values[i], fetched[slots_of[start + i]], preferred_element_type=F32)
            row = jnp.where(start + i < count[0], rows_of[start + i], row_blocks)
            total[row] += product


def tile_sum(plan, count, rows_of, slots_of, values, fetched):
    tiles, tile, width = values.shape[0], values.shape[1], fetched.shape[2]
    grid_spec = pltpu.PrefetchScalarGridSpec(
        num_scalar_prefetch=3,
        grid=(tiles // BATCH,),
        in_specs=[
            pl.BlockSpec(
                (BATCH, tile, tile), lambda i, count, *_: (jnp.minimum(i, lax.div(count[0] - 1, BATCH)), 0, 0)
            ),
            pl.BlockSpec(fetched.shape, lambda i, *_: (0, 0, 0)),
        ],
        out_specs=pl.BlockSpec((plan.blocks + 1, tile, width), lambda i, *_: (0, 0, 0)),
    )
    return pl.pallas_call(
        functools.partial(tile_kernel, plan.blocks),
        out_shape=jax.ShapeDtypeStruct((plan.blocks + 1, tile, width), F32),
        grid_spec=grid_spec,
        compiler_params=pltpu.CompilerParams(
            vmem_limit_bytes=40 << 20, dimension_semantics=("arbitrary",)
        ),
        name="tile_sum",
    )(count, rows_of, slots_of, values, fetched)


def on_device(
    features, tile_values, tile_rows, tile_slots, tile_counts, fetch_lists, filter_weights
):
    values, rows_of, slots_of = tile_values[0, 0], tile_rows[0, 0], tile_slots[0, 0]
    count, wanted = tile_counts[0], fetch_lists[0]
    tile, width = values.shape[1], features.shape[1]
    n, per_peer = wanted.shape
    blocks = features.shape[0] // tile
    plan = Plan(n, lax.axis_size("rep"), blocks, per_peer)
    share, chips, portion = plan.share, plan.chips, plan.portion
    dma = pltpu.SemaphoreType.DMA
    vmem, smem = pl.BlockSpec(memory_space=pltpu.VMEM), pl.BlockSpec(memory_space=pltpu.SMEM)
    lists = jnp.pad(wanted[:, None, :], ((0, 0), (0, 7), (0, 128 - per_peer)))
    field = features.reshape(blocks, tile, width)
    fetched_shape = jax.ShapeDtypeStruct((n * per_peer, tile, width), BF16)
    share_shape = jax.ShapeDtypeStruct((share, tile, width), BF16)
    exchange_scratch = [dma((2, n)), dma((2, n, chips)), dma((2, n, chips))]
    stage = pltpu.VMEM((n - 1, portion, tile, width), BF16)
    reduce_buffers = [
        pltpu.VMEM((chips, share, tile, width), F32),
        pltpu.VMEM((chips - 1, share, tile, width), BF16),
        pltpu.VMEM((chips - 1, share, tile, width), BF16),
    ]
    pairs = dma((2, chips))

    def params(number):
        return pltpu.CompilerParams(
            collective_id=number, has_side_effects=True, vmem_limit_bytes=32 << 20
        )

    fetched, served = pl.pallas_call(
        functools.partial(first_kernel, plan),
        out_shape=(fetched_shape, jax.ShapeDtypeStruct(lists.shape, jnp.int32)),
        in_specs=[vmem, vmem],
        out_specs=(vmem, smem),
        scratch_shapes=[
            pltpu.VMEM(lists.shape, jnp.int32), stage, dma((2, n)), *exchange_scratch, dma(()),
        ],
        compiler_params=params(0),
        name="first_fetch",
    )(lists, field)
    own = [lax.dynamic_slice_in_dim(field, lax.axis_index("rep") * share, share, 0)]
    last = filter_weights.shape[0] - 1
    for degree in range(1, last + 1):
        partial = tile_sum(plan, count, rows_of, slots_of, values, fetched)
        previous = own[max(degree - 2, 0)]
        if degree < last:
            fetched, term = pl.pallas_call(
                functools.partial(middle_kernel, plan, degree),
                out_shape=(fetched_shape, share_shape),
                in_specs=[vmem, vmem, smem],
                out_specs=(vmem, vmem),
                scratch_shapes=[
                    *reduce_buffers, pltpu.VMEM(field.shape, BF16), stage,
                    pairs, pairs, pairs, pairs, *exchange_scratch,
                ],
                compiler_params=params(degree),
                name=f"reduce_and_fetch_{degree}",
            )(partial, previous, served)
        else:
            term = pl.pallas_call(
                functools.partial(last_kernel, plan, degree),
                out_shape=share_shape,
                in_specs=[vmem, vmem],
                out_specs=vmem,
                scratch_shapes=[*reduce_buffers, pairs, pairs],
                compiler_params=params(degree),
                name="reduce_last",
            )(partial, previous)
        own.append(term)
    joined = jnp.concatenate([t.reshape(share * tile, width) for t in own], axis=1)
    flat = filter_weights.reshape(-1, filter_weights.shape[2])
    return jnp.dot(joined, flat, preferred_element_type=F32).astype(BF16)


def solution(mesh):
    return jax.shard_map(
        on_device,
        mesh=mesh,
        in_specs=(
            P("rows", None),
            P("rows", "rep", None, None, None),
            P("rows", "rep", None),
            P("rows", "rep", None),
            P("rows", "rep"),
            P("rows", None, None),
            P(),
        ),
        out_specs=P(("rows", "rep"), None),
        check_vma=False,
    )
```

```python
import functools

import jax
import jax.numpy as jnp
from jax import lax
from jax.experimental import pallas as pl
from jax.experimental.pallas import tpu as pltpu
from jax.sharding import PartitionSpec as P

CHUNK, UNROLL, HELD, WINDOW = 32, 16, 4, 3
PIECES = 2
MESH = pl.DeviceIdType.MESH
F32, BF16 = jnp.float32, jnp.bfloat16


class Plan:
    def __init__(self, n_rows, n_rep, row_blocks, per_peer):
        self.n, self.reps, self.chips = n_rows, n_rep, n_rep // 2
        self.blocks, self.peer = row_blocks, per_peer
        self.share, self.portion = row_blocks // n_rep, per_peer // n_rep

    def place(self):
        self.r, self.j = lax.axis_index("rows"), lax.axis_index("rep")
        self.c, self.x = lax.rem(self.j, 2), lax.div(self.j, 2)
        self.sib = self.j + 1 - 2 * self.c

    def chip(self, e):
        return lax.rem(self.x + e + self.chips, self.chips)

    def rank(self, e):
        return self.chip(e) * 2 + self.c

    def row(self, d):
        return self.r ^ d

    def order(self):
        half = self.n // 2
        return [d for k in range(half) for d in (half + k, k) if d]


def remote(src, dst, send, recv, target):
    copy = pltpu.make_async_remote_copy(
        src_ref=src, dst_ref=dst, send_sem=send, recv_sem=recv, device_id=target, device_id_type=MESH
    )
    copy.start()
    return copy


def greet(plan, with_rows):
    barrier = pltpu.get_barrier_semaphore()
    targets = [(plan.r, plan.sib)] + [(plan.r, plan.rank(e)) for e in range(1, plan.chips)]
    if with_rows:
        targets += [(plan.row(d), plan.j) for d in plan.order()]
    for target in targets:
        pl.semaphore_signal(barrier, inc=1, device_id=target, device_id_type=MESH)
    pl.semaphore_wait(barrier, len(targets))


def exchange(plan, full, served, fetched, stage, sems):
    ex, fx, fc = sems
    n, chips, portion, peer = plan.n, plan.chips, plan.portion, plan.peer
    sent, across, beside = {}, {}, {}
    order = plan.order()

    def send(d):
        to = plan.row(d)
        for i in range(portion):
            stage[d - 1, i] = full[served[to, 0, plan.j * portion + i]]
        sent[d] = remote(
            stage.at[d - 1],
            fetched.at[pl.ds(plan.r * peer + plan.j * portion, portion)],
            ex.at[0, d],
            ex.at[1, d],
            (to, plan.j),
        )

    def segment(d, rank):
        return fetched.at[pl.ds(plan.row(d) * peer + rank * portion, portion)]

    def pass_beside(d):
        for e in range(1, chips):
            across[d, e].wait_recv()
            seg = segment(d, plan.rank(-e))
            beside[d, e] = remote(seg, seg, fc.at[0, d, e], fc.at[1, d, e], (plan.r, plan.sib))

    for d in order[:WINDOW]:
        send(d)
    for s in range(peer):
        fetched[plan.r * peer + s] = full[served[plan.r, 0, s]]
    for k, d in enumerate(order):
        sent[d].wait_recv()
        seg = segment(d, plan.j)
        for e in range(1, chips):
            across[d, e] = remote(seg, seg, fx.at[0, d, e], fx.at[1, d, e], (plan.r, plan.rank(e)))
        if k + WINDOW < len(order):
            send(order[k + WINDOW])
        beside[d, 0] = remote(seg, seg, fc.at[0, d, 0], fc.at[1, d, 0], (plan.r, plan.sib))
    for d in order:
        pass_beside(d)
    for copy in beside.values():
        copy.wait_recv()
    for copies in (sent, across, beside):
        for copy in copies.values():
            copy.wait_send()


def first_kernel(
    plan, wanted, full, values, meta, fetched, served, moved, meta_beside,
    lists, stage, ls, ex, fx, fc, local, ms, mm,
):
    plan.place()
    greet(plan, True)
    copies = [
        remote(wanted.at[plan.row(d)], lists.at[plan.r], ls.at[0, d], ls.at[1, d], (plan.row(d), plan.j))
        for d in plan.order()
    ]
    handed = [
        remote(values.at[k, 1], moved.at[k], ms.at[0, k], ms.at[1, k], (plan.r, plan.sib))
        for k in range(values.shape[0])
    ]
    handed.append(remote(meta, meta_beside, mm.at[0], mm.at[1], (plan.r, plan.sib)))
    lists[plan.r] = wanted[plan.r]
    for copy in copies:
        copy.wait_recv()
    inner = pltpu.make_async_copy(lists, served, local)
    inner.start()
    inner.wait()
    exchange(plan, full, served, fetched, stage, (ex, fx, fc))
    for copy in copies:
        copy.wait_send()
    for copy in handed:
        copy.wait()


def sum_all(plan, degree, partial, previous, core_in, chip_out, x_in, cs, xs, ac, full):
    chips, parts = plan.chips, plan.chips * PIECES
    group = plan.share // PIECES
    core, cross, beside = [], [], []

    def base(k, c):
        return (k // PIECES * 2 + c) * plan.share + k % PIECES * group

    for k in range(parts):
        src = partial.at[pl.ds(base(k, 1 - plan.c), group)]
        core.append(remote(src, core_in.at[k], cs.at[0, k], cs.at[1, k], (plan.r, plan.sib)))
    for k in range(parts):
        core[k].wait_recv()

        @pl.loop(0, group)
        def _(b):
            both = partial[base(k, plan.c) + b] + core_in[k, b]
            core_in[k, b] = both
            chip_out[k, b] = both.astype(BF16)

        cross.append([
            remote(
                chip_out.at[k], x_in.at[e - 1, k], xs.at[0, e, k], xs.at[1, e, k], (plan.r, plan.rank(e))
            )
            for e in range(1, chips)
        ])
    for k in range(parts):
        for copy in cross[k]:
            copy.wait_recv()

        @pl.loop(0, group)
        def _(b):
            total = core_in[k, b]
            for e in range(1, chips):
                total = total + x_in[e - 1, k, b].astype(F32)
            if degree > 1:
                total = 2.0 * total - previous[base(k, plan.c) + b].astype(F32)
            full[base(k, plan.c) + b] = total.astype(BF16)

        part = full.at[pl.ds(base(k, plan.c), group)]
        beside.append(remote(part, part, ac.at[0, k], ac.at[1, k], (plan.r, plan.sib)))
    for copy in beside:
        copy.wait_recv()
    return [*core, *beside, *[copy for copies in cross for copy in copies]]


def middle_kernel(
    plan, degree, partial, previous, served, fetched, full, core_in, chip_out, x_in, stage, cs, xs, ac, ex, fx, fc
):
    plan.place()
    greet(plan, True)
    pending = sum_all(plan, degree, partial, previous, core_in, chip_out, x_in, cs, xs, ac, full)
    exchange(plan, full, served, fetched, stage, (ex, fx, fc))
    for copy in pending:
        copy.wait_send()


def last_kernel(plan, partial, *refs):
    count = len(refs) - 8
    terms, (weights, out, core_in, chip_out, x_in, filtered, cs, xs) = refs[:count], refs[count:]
    plan.place()
    greet(plan, False)
    share, chips = plan.share, plan.chips
    core, cross = {}, {}
    for e in [*range(1, chips), 0]:
        src = partial.at[pl.ds((plan.chip(e) * 2 + 1 - plan.c) * share, share)]
        core[e] = remote(src, core_in.at[e], cs.at[0, e], cs.at[1, e], (plan.r, plan.sib))
    for e in range(1, chips):
        core[e].wait_recv()

        @pl.loop(0, share)
        def _(b):
            chip_out[e - 1, b] = (partial[plan.rank(e) * share + b] + core_in[e, b]).astype(BF16)

        cross[e] = remote(
            chip_out.at[e - 1], x_in.at[e - 1], xs.at[0, e], xs.at[1, e], (plan.r, plan.rank(e))
        )

    @pl.loop(0, share)
    def _(b):
        filtered[b] = sum(
            jnp.dot(term[plan.j * share + b], weights[k], preferred_element_type=F32)
            for k, term in enumerate(terms)
        )

    for copy in [core[0], *cross.values()]:
        copy.wait_recv()

    @pl.loop(0, share)
    def _(b):
        total = partial[plan.j * share + b] + core_in[0, b]
        for e in range(1, chips):
            total = total + x_in[e - 1, b].astype(F32)
        if count > 1:
            total = 2.0 * total - terms[-2][plan.j * share + b].astype(F32)
        new = jnp.dot(total.astype(BF16), weights[count], preferred_element_type=F32)
        out[b] = (filtered[b] + new).astype(BF16)

    for copy in [*core.values(), *cross.values()]:
        copy.wait_send()


def live(meta, tiles):
    return meta[2 * (tiles // 128), 0]


def tile_kernel(row_blocks, tiles, mine, theirs, own, moved, fetched, total):
    step = pl.program_id(0)
    lines = tiles // 128

    @pl.when(step == 0)
    def _():
        @pl.loop(0, row_blocks + 1)
        def _(b):
            total[b] = jnp.zeros(total.shape[1:], F32)

    def add(meta, values, start):
        count = live(meta, tiles)
        line, lane = lax.div(start, 128), lax.rem(start, 128)

        @pl.when(start < count)
        def _():
            @pl.loop(0, CHUNK // UNROLL)
            def _(part):
                for first in range(0, UNROLL, HELD):
                    places = [part * UNROLL + first + i for i in range(HELD)]
                    products = [
                        jnp.dot(values[t], fetched[meta[lines + line, lane + t]], preferred_element_type=F32)
                        for t in places
                    ]
                    for t, product in zip(places, products):
                        row = jnp.where(start + t < count, meta[line, lane + t], row_blocks)
                        total[row] += product

    add(mine, own, step * 2 * CHUNK)
    add(theirs, moved, step * 2 * CHUNK + CHUNK)


def tile_sum(plan, mine, theirs, values, moved, fetched):
    steps, tile, width = values.shape[0], values.shape[-1], fetched.shape[2]
    tiles = steps * 2 * CHUNK

    def own_place(i, mine, theirs):
        return jnp.minimum(i, lax.div(live(mine, tiles) - 1, 2 * CHUNK)), 0, 0, 0, 0

    def moved_place(i, mine, theirs):
        return jnp.minimum(i, lax.div(jnp.maximum(live(theirs, tiles) - CHUNK - 1, 0), 2 * CHUNK)), 0, 0, 0

    grid_spec = pltpu.PrefetchScalarGridSpec(
        num_scalar_prefetch=2,
        grid=(steps,),
        in_specs=[
            pl.BlockSpec((None, None, CHUNK, tile, tile), own_place),
            pl.BlockSpec((None, CHUNK, tile, tile), moved_place),
            pl.BlockSpec(fetched.shape, lambda i, *_: (0, 0, 0)),
        ],
        out_specs=pl.BlockSpec((plan.blocks + 1, tile, width), lambda i, *_: (0, 0, 0)),
    )
    return pl.pallas_call(
        functools.partial(tile_kernel, plan.blocks, tiles),
        out_shape=jax.ShapeDtypeStruct((plan.blocks + 1, tile, width), F32),
        grid_spec=grid_spec,
        compiler_params=pltpu.CompilerParams(
            vmem_limit_bytes=40 << 20, dimension_semantics=("arbitrary",)
        ),
        name="tile_sum",
    )(mine, theirs, values, moved, fetched)


def on_device(
    features, tile_values, tile_rows, tile_slots, tile_counts, fetch_lists, filter_weights
):
    wanted, tiles, tile, width = fetch_lists[0], tile_values.shape[2], tile_values.shape[3], features.shape[1]
    values = tile_values.reshape(tiles // (2 * CHUNK), 2, CHUNK, tile, tile)
    n, per_peer = wanted.shape
    blocks = features.shape[0] // tile
    plan = Plan(n, lax.axis_size("rep"), blocks, per_peer)
    share, chips, portion = plan.share, plan.chips, plan.portion
    parts, group, outs = chips * PIECES, plan.share // PIECES, filter_weights.shape[2]
    dma = pltpu.SemaphoreType.DMA
    vmem, smem, hbm = (pl.BlockSpec(memory_space=m) for m in (pltpu.VMEM, pltpu.SMEM, pltpu.HBM))
    lists = jnp.pad(wanted[:, None, :], ((0, 0), (0, 7), (0, 128 - per_peer)))
    lines = tiles // 128
    meta = jnp.concatenate([
        tile_rows.reshape(lines, 128),
        tile_slots.reshape(lines, 128),
        jnp.broadcast_to(tile_counts, (8, 128)),
    ])
    field = features.reshape(blocks, tile, width)
    fetched_shape = jax.ShapeDtypeStruct((n * per_peer, tile, width), BF16)
    moved_shape = jax.ShapeDtypeStruct((values.shape[0], CHUNK, tile, tile), BF16)
    exchange_scratch = [dma((2, n)), dma((2, n, chips)), dma((2, n, chips))]
    stage = pltpu.VMEM((n - 1, portion, tile, width), BF16)

    def params(number):
        return pltpu.CompilerParams(
            collective_id=number, has_side_effects=True, vmem_limit_bytes=32 << 20
        )

    fetched, served, moved, meta_beside = pl.pallas_call(
        functools.partial(first_kernel, plan),
        out_shape=(
            fetched_shape,
            jax.ShapeDtypeStruct(lists.shape, jnp.int32),
            moved_shape,
            jax.ShapeDtypeStruct(meta.shape, jnp.int32),
        ),
        in_specs=[vmem, vmem, hbm, vmem],
        out_specs=(vmem, smem, hbm, vmem),
        scratch_shapes=[
            pltpu.VMEM(lists.shape, jnp.int32), stage, dma((2, n)), *exchange_scratch, dma(()),
            dma((2, values.shape[0])), dma((2,)),
        ],
        compiler_params=params(0),
        name="first_fetch",
    )(lists, field, values, meta)
    terms = [field]
    last = filter_weights.shape[0] - 1
    for degree in range(1, last + 1):
        partial = tile_sum(plan, meta, meta_beside, values, moved, fetched)
        if degree < last:
            fetched, term = pl.pallas_call(
                functools.partial(middle_kernel, plan, degree),
                out_shape=(fetched_shape, jax.ShapeDtypeStruct(field.shape, BF16)),
                in_specs=[vmem, vmem, smem],
                out_specs=(vmem, vmem),
                scratch_shapes=[
                    pltpu.VMEM((parts, group, tile, width), F32),
                    pltpu.VMEM((parts, group, tile, width), BF16),
                    pltpu.VMEM((chips - 1, parts, group, tile, width), BF16),
                    stage, dma((2, parts)), dma((2, chips, parts)), dma((2, parts)), *exchange_scratch,
                ],
                compiler_params=params(degree),
                name=f"reduce_and_fetch_{degree}",
            )(partial, terms[max(degree - 2, 0)], served)
            terms.append(term)
    out = pl.pallas_call(
        functools.partial(last_kernel, plan),
        out_shape=jax.ShapeDtypeStruct((share, tile, outs), BF16),
        in_specs=[vmem] * (len(terms) + 2),
        out_specs=vmem,
        scratch_shapes=[
            pltpu.VMEM((chips, share, tile, width), F32),
            pltpu.VMEM((chips - 1, share, tile, width), BF16),
            pltpu.VMEM((chips - 1, share, tile, width), BF16),
            pltpu.VMEM((share, tile, outs), F32),
            dma((2, chips)),
            dma((2, chips)),
        ],
        compiler_params=params(last),
        name="reduce_last",
    )(partial, *terms, filter_weights)
    return out.reshape(share * tile, outs)


def solution(mesh):
    return jax.shard_map(
        on_device,
        mesh=mesh,
        in_specs=(
            P("rows", None),
            P("rows", "rep", None, None, None),
            P("rows", "rep", None),
            P("rows", "rep", None),
            P("rows", "rep"),
            P("rows", None, None),
            P(),
        ),
        out_specs=P(("rows", "rep"), None),
        check_vma=False,
    )
```

```python
import functools

import jax
import jax.numpy as jnp
from jax import lax
from jax.experimental import pallas as pl
from jax.experimental.pallas import tpu as pltpu
from jax.sharding import PartitionSpec as P

CHUNK, UNROLL, HELD, WINDOW = 32, 16, 4, 15
PIECES = 2
MESH = pl.DeviceIdType.MESH
F32, BF16 = jnp.float32, jnp.bfloat16


class Plan:
    def __init__(self, n_rows, n_rep, row_blocks, per_peer):
        self.n, self.reps, self.chips = n_rows, n_rep, n_rep // 2
        self.blocks, self.peer = row_blocks, per_peer
        self.share, self.portion = row_blocks // n_rep, per_peer // n_rep

    def place(self):
        self.r, self.j = lax.axis_index("rows"), lax.axis_index("rep")
        self.c, self.x = lax.rem(self.j, 2), lax.div(self.j, 2)
        self.sib = self.j + 1 - 2 * self.c

    def chip(self, e):
        return lax.rem(self.x + e + self.chips, self.chips)

    def rank(self, e):
        return self.chip(e) * 2 + self.c

    def row(self, d):
        return self.r ^ d

    def order(self):
        half = self.n // 2
        return [d for k in range(half) for d in (half + k, k) if d]


def remote(src, dst, send, recv, target):
    copy = pltpu.make_async_remote_copy(
        src_ref=src, dst_ref=dst, send_sem=send, recv_sem=recv, device_id=target, device_id_type=MESH
    )
    copy.start()
    return copy


def greet(plan, with_rows):
    barrier = pltpu.get_barrier_semaphore()
    targets = [(plan.r, plan.sib)] + [(plan.r, plan.rank(e)) for e in range(1, plan.chips)]
    if with_rows:
        targets += [(plan.row(d), plan.j) for d in plan.order()]
    for target in targets:
        pl.semaphore_signal(barrier, inc=1, device_id=target, device_id_type=MESH)
    pl.semaphore_wait(barrier, len(targets))


def exchange(plan, full, served, fetched, stage, sems):
    ex, fx, fc = sems
    n, chips, portion, peer = plan.n, plan.chips, plan.portion, plan.peer
    sent, across, beside = {}, {}, {}
    order = plan.order()

    def reach(d):
        return (peer // 2, plan.c * (peer // 2)) if d < n // 2 else (portion, plan.j * portion)

    def send(d):
        to = plan.row(d)
        size, first = reach(d)
        for i in range(size):
            stage[d - 1, i] = full[served[to, 0, first + i]]
        sent[d] = remote(
            stage.at[d - 1, pl.ds(0, size)],
            fetched.at[pl.ds(plan.r * peer + first, size)],
            ex.at[0, d],
            ex.at[1, d],
            (to, plan.j),
        )

    def segment(d, rank):
        return fetched.at[pl.ds(plan.row(d) * peer + rank * portion, portion)]

    far = [d for d in order if d >= n // 2]

    def pass_beside(d):
        for e in range(1, chips):
            across[d, e].wait_recv()
            seg = segment(d, plan.rank(-e))
            beside[d, e] = remote(seg, seg, fc.at[0, d, e], fc.at[1, d, e], (plan.r, plan.sib))

    for d in order[:WINDOW]:
        send(d)
    for s in range(peer):
        fetched[plan.r * peer + s] = full[served[plan.r, 0, s]]
    for k, d in enumerate(order):
        sent[d].wait_recv()
        size, first = reach(d)
        seg = fetched.at[pl.ds(plan.row(d) * peer + first, size)]
        for e in range(1, chips if d in far else 1):
            across[d, e] = remote(seg, seg, fx.at[0, d, e], fx.at[1, d, e], (plan.r, plan.rank(e)))
        if k + WINDOW < len(order):
            send(order[k + WINDOW])
        beside[d, 0] = remote(seg, seg, fc.at[0, d, 0], fc.at[1, d, 0], (plan.r, plan.sib))
    for d in far:
        pass_beside(d)
    for copy in beside.values():
        copy.wait_recv()
    for copies in (sent, across, beside):
        for copy in copies.values():
            copy.wait_send()


def first_kernel(
    plan, wanted, full, values, meta, fetched, served, moved, meta_beside,
    lists, stage, ls, ex, fx, fc, local, ms, mm,
):
    plan.place()
    greet(plan, True)
    copies = [
        remote(wanted.at[plan.row(d)], lists.at[plan.r], ls.at[0, d], ls.at[1, d], (plan.row(d), plan.j))
        for d in plan.order()
    ]
    handed = [
        remote(values.at[k, 1], moved.at[k], ms.at[0, k], ms.at[1, k], (plan.r, plan.sib))
        for k in range(values.shape[0])
    ]
    handed.append(remote(meta, meta_beside, mm.at[0], mm.at[1], (plan.r, plan.sib)))
    lists[plan.r] = wanted[plan.r]
    for copy in copies:
        copy.wait_recv()
    inner = pltpu.make_async_copy(lists, served, local)
    inner.start()
    inner.wait()
    exchange(plan, full, served, fetched, stage, (ex, fx, fc))
    for copy in copies:
        copy.wait_send()
    for copy in handed:
        copy.wait()


def sum_all(plan, degree, partial, previous, core_in, chip_out, x_in, cs, xs, ac, full):
    chips, parts = plan.chips, plan.chips * PIECES
    group = plan.share // PIECES
    core, cross, beside = [], [], []

    def base(k, c):
        return (k // PIECES * 2 + c) * plan.share + k % PIECES * group

    for k in range(parts):
        src = partial.at[pl.ds(base(k, 1 - plan.c), group)]
        core.append(remote(src, core_in.at[k], cs.at[0, k], cs.at[1, k], (plan.r, plan.sib)))
    for k in range(parts):
        core[k].wait_recv()

        @pl.loop(0, group)
        def _(b):
            both = partial[base(k, plan.c) + b] + core_in[k, b]
            core_in[k, b] = both
            chip_out[k, b] = both.astype(BF16)

        cross.append([
            remote(
                chip_out.at[k], x_in.at[e - 1, k], xs.at[0, e, k], xs.at[1, e, k], (plan.r, plan.rank(e))
            )
            for e in range(1, chips)
        ])
    for k in range(parts):
        for copy in cross[k]:
            copy.wait_recv()

        @pl.loop(0, group)
        def _(b):
            total = core_in[k, b]
            for e in range(1, chips):
                total = total + x_in[e - 1, k, b].astype(F32)
            if degree > 1:
                total = 2.0 * total - previous[base(k, plan.c) + b].astype(F32)
            full[base(k, plan.c) + b] = total.astype(BF16)

        part = full.at[pl.ds(base(k, plan.c), group)]
        beside.append(remote(part, part, ac.at[0, k], ac.at[1, k], (plan.r, plan.sib)))
    for copy in beside:
        copy.wait_recv()
    return [*core, *beside, *[copy for copies in cross for copy in copies]]


def middle_kernel(
    plan, degree, partial, previous, served, fetched, full, core_in, chip_out, x_in, stage, cs, xs, ac, ex, fx, fc
):
    plan.place()
    greet(plan, True)
    pending = sum_all(plan, degree, partial, previous, core_in, chip_out, x_in, cs, xs, ac, full)
    exchange(plan, full, served, fetched, stage, (ex, fx, fc))
    for copy in pending:
        copy.wait_send()


def last_kernel(plan, partial, *refs):
    count = len(refs) - 8
    terms, (weights, out, core_in, chip_out, x_in, filtered, cs, xs) = refs[:count], refs[count:]
    plan.place()
    greet(plan, False)
    share, chips = plan.share, plan.chips
    core, cross = {}, {}
    for e in [*range(1, chips), 0]:
        src = partial.at[pl.ds((plan.chip(e) * 2 + 1 - plan.c) * share, share)]
        core[e] = remote(src, core_in.at[e], cs.at[0, e], cs.at[1, e], (plan.r, plan.sib))
    for e in range(1, chips):
        core[e].wait_recv()

        @pl.loop(0, share)
        def _(b):
            chip_out[e - 1, b] = (partial[plan.rank(e) * share + b] + core_in[e, b]).astype(BF16)

        cross[e] = remote(
            chip_out.at[e - 1], x_in.at[e - 1], xs.at[0, e], xs.at[1, e], (plan.r, plan.rank(e))
        )

    @pl.loop(0, share)
    def _(b):
        filtered[b] = sum(
            jnp.dot(term[plan.j * share + b], weights[k], preferred_element_type=F32)
            for k, term in enumerate(terms)
        )

    for copy in [core[0], *cross.values()]:
        copy.wait_recv()

    @pl.loop(0, share)
    def _(b):
        total = partial[plan.j * share + b] + core_in[0, b]
        for e in range(1, chips):
            total = total + x_in[e - 1, b].astype(F32)
        if count > 1:
            total = 2.0 * total - terms[-2][plan.j * share + b].astype(F32)
        new = jnp.dot(total.astype(BF16), weights[count], preferred_element_type=F32)
        out[b] = (filtered[b] + new).astype(BF16)

    for copy in [*core.values(), *cross.values()]:
        copy.wait_send()


def live(meta, tiles):
    return meta[2 * (tiles // 128), 0]


def tile_kernel(row_blocks, tiles, mine, theirs, own, moved, fetched, total):
    step = pl.program_id(0)
    lines = tiles // 128

    @pl.when(step == 0)
    def _():
        @pl.loop(0, row_blocks + 1)
        def _(b):
            total[b] = jnp.zeros(total.shape[1:], F32)

    def add(meta, values, start):
        count = live(meta, tiles)
        line, lane = lax.div(start, 128), lax.rem(start, 128)

        @pl.when(start < count)
        def _():
            @pl.loop(0, CHUNK // UNROLL)
            def _(part):
                for first in range(0, UNROLL, HELD):
                    places = [part * UNROLL + first + i for i in range(HELD)]
                    products = [
                        jnp.dot(values[t], fetched[meta[lines + line, lane + t]], preferred_element_type=F32)
                        for t in places
                    ]
                    for t, product in zip(places, products):
                        row = jnp.where(start + t < count, meta[line, lane + t], row_blocks)
                        total[row] += product

    add(mine, own, step * 2 * CHUNK)
    add(theirs, moved, step * 2 * CHUNK + CHUNK)


def tile_sum(plan, mine, theirs, values, moved, fetched):
    steps, tile, width = values.shape[0], values.shape[-1], fetched.shape[2]
    tiles = steps * 2 * CHUNK

    def own_place(i, mine, theirs):
        return jnp.minimum(i, lax.div(live(mine, tiles) - 1, 2 * CHUNK)), 0, 0, 0, 0

    def moved_place(i, mine, theirs):
        return jnp.minimum(i, lax.div(jnp.maximum(live(theirs, tiles) - CHUNK - 1, 0), 2 * CHUNK)), 0, 0, 0

    grid_spec = pltpu.PrefetchScalarGridSpec(
        num_scalar_prefetch=2,
        grid=(steps,),
        in_specs=[
            pl.BlockSpec((None, None, CHUNK, tile, tile), own_place),
            pl.BlockSpec((None, CHUNK, tile, tile), moved_place),
            pl.BlockSpec(fetched.shape, lambda i, *_: (0, 0, 0)),
        ],
        out_specs=pl.BlockSpec((plan.blocks + 1, tile, width), lambda i, *_: (0, 0, 0)),
    )
    return pl.pallas_call(
        functools.partial(tile_kernel, plan.blocks, tiles),
        out_shape=jax.ShapeDtypeStruct((plan.blocks + 1, tile, width), F32),
        grid_spec=grid_spec,
        compiler_params=pltpu.CompilerParams(
            vmem_limit_bytes=40 << 20, dimension_semantics=("arbitrary",)
        ),
        name="tile_sum",
    )(mine, theirs, values, moved, fetched)


def on_device(
    features, tile_values, tile_rows, tile_slots, tile_counts, fetch_lists, filter_weights
):
    wanted, tiles, tile, width = fetch_lists[0], tile_values.shape[2], tile_values.shape[3], features.shape[1]
    values = tile_values.reshape(tiles // (2 * CHUNK), 2, CHUNK, tile, tile)
    n, per_peer = wanted.shape
    blocks = features.shape[0] // tile
    plan = Plan(n, lax.axis_size("rep"), blocks, per_peer)
    share, chips, portion = plan.share, plan.chips, plan.portion
    parts, group, outs = chips * PIECES, plan.share // PIECES, filter_weights.shape[2]
    dma = pltpu.SemaphoreType.DMA
    vmem, smem, hbm = (pl.BlockSpec(memory_space=m) for m in (pltpu.VMEM, pltpu.SMEM, pltpu.HBM))
    lists = jnp.pad(wanted[:, None, :], ((0, 0), (0, 7), (0, 128 - per_peer)))
    lines = tiles // 128
    meta = jnp.concatenate([
        tile_rows.reshape(lines, 128),
        tile_slots.reshape(lines, 128),
        jnp.broadcast_to(tile_counts, (8, 128)),
    ])
    field = features.reshape(blocks, tile, width)
    fetched_shape = jax.ShapeDtypeStruct((n * per_peer, tile, width), BF16)
    moved_shape = jax.ShapeDtypeStruct((values.shape[0], CHUNK, tile, tile), BF16)
    exchange_scratch = [dma((2, n)), dma((2, n, chips)), dma((2, n, chips))]
    stage = pltpu.VMEM((n - 1, per_peer // 2, tile, width), BF16)

    def params(number):
        return pltpu.CompilerParams(
            collective_id=number, has_side_effects=True, vmem_limit_bytes=32 << 20
        )

    fetched, served, moved, meta_beside = pl.pallas_call(
        functools.partial(first_kernel, plan),
        out_shape=(
            fetched_shape,
            jax.ShapeDtypeStruct(lists.shape, jnp.int32),
            moved_shape,
            jax.ShapeDtypeStruct(meta.shape, jnp.int32),
        ),
        in_specs=[vmem, vmem, hbm, vmem],
        out_specs=(vmem, smem, hbm, vmem),
        scratch_shapes=[
            pltpu.VMEM(lists.shape, jnp.int32), stage, dma((2, n)), *exchange_scratch, dma(()),
            dma((2, values.shape[0])), dma((2,)),
        ],
        compiler_params=params(0),
        name="first_fetch",
    )(lists, field, values, meta)
    terms = [field]
    last = filter_weights.shape[0] - 1
    for degree in range(1, last + 1):
        partial = tile_sum(plan, meta, meta_beside, values, moved, fetched)
        if degree < last:
            fetched, term = pl.pallas_call(
                functools.partial(middle_kernel, plan, degree),
                out_shape=(fetched_shape, jax.ShapeDtypeStruct(field.shape, BF16)),
                in_specs=[vmem, vmem, smem],
                out_specs=(vmem, vmem),
                scratch_shapes=[
                    pltpu.VMEM((parts, group, tile, width), F32),
                    pltpu.VMEM((parts, group, tile, width), BF16),
                    pltpu.VMEM((chips - 1, parts, group, tile, width), BF16),
                    stage, dma((2, parts)), dma((2, chips, parts)), dma((2, parts)), *exchange_scratch,
                ],
                compiler_params=params(degree),
                name=f"reduce_and_fetch_{degree}",
            )(partial, terms[max(degree - 2, 0)], served)
            terms.append(term)
    out = pl.pallas_call(
        functools.partial(last_kernel, plan),
        out_shape=jax.ShapeDtypeStruct((share, tile, outs), BF16),
        in_specs=[vmem] * (len(terms) + 2),
        out_specs=vmem,
        scratch_shapes=[
            pltpu.VMEM((chips, share, tile, width), F32),
            pltpu.VMEM((chips - 1, share, tile, width), BF16),
            pltpu.VMEM((chips - 1, share, tile, width), BF16),
            pltpu.VMEM((share, tile, outs), F32),
            dma((2, chips)),
            dma((2, chips)),
        ],
        compiler_params=params(last),
        name="reduce_last",
    )(partial, *terms, filter_weights)
    return out.reshape(share * tile, outs)


def solution(mesh):
    return jax.shard_map(
        on_device,
        mesh=mesh,
        in_specs=(
            P("rows", None),
            P("rows", "rep", None, None, None),
            P("rows", "rep", None),
            P("rows", "rep", None),
            P("rows", "rep"),
            P("rows", None, None),
            P(),
        ),
        out_specs=P(("rows", "rep"), None),
        check_vma=False,
    )
```
